32 devices in a mesh: sec: 4 (over y, core), blk: 2 (over x), gy: 4 (over z).
Axes of the slice: x: 2, y: 2, z: 4, core: 2. Of those that a mesh axis runs over, the one named last changes fastest.
Arguments:
- normalized_kelvin: float32 [32, 64, 512], P('blk', 'gy', 'sec'), may hold values from 0.6 to 2
- co2_molar_part: float32 [32, 64, 512], P('blk', 'gy', 'sec'), may hold values from 0.02 to 0.2
- h2o_molar_part: float32 [32, 64, 512], P('blk', 'gy', 'sec'), may hold values from 0.02 to 0.25
- particulate_scaled: float32 [32, 64, 512], P('blk', 'gy', 'sec'), may hold values from 0.01 to 1
- region_local_subgrids: int32 [4, 2, 4, 512], P('sec', 'blk', 'gy'), may hold values from 0 to 511, each once within a row
- entry_target_tile: int32 [64, 5], P(('sec', 'blk', 'gy')), may hold values from 0 to 63, as said below
- nonempty_entries_per_strip: int32 [64], P(('sec', 'blk', 'gy')), may hold values from 1 to 5, as said below
- transfer_matrix_tiles: bfloat16 [64, 5, 256, 256], P(('sec', 'blk', 'gy')), may hold values from -0.15625 to 0.15625
Outputs:
- temperature_new: float32 [32, 64, 512], P('blk', 'gy', 'sec')
- carbon_dioxide_new: float32 [32, 64, 512], P('blk', 'gy', 'sec')
- water_new: float32 [32, 64, 512], P('blk', 'gy', 'sec')
- soot_new: float32 [32, 64, 512], P('blk', 'gy', 'sec')
- source: float32 [32, 64, 512], P('blk', 'gy', 'sec')
The draws below stay inside these ranges and needn't reach their ends.
Inputs may be any that keep to these rules, and one draw needn't show every extreme that they name: `region_local_subgrids`: each device's row is a permutation of its 512 boxes. `entry_target_tile`: slot 0 of block row r names r itself; slots at or beyond the row's count are not read. `nonempty_entries_per_strip`: some block row has 5 live slots and some has 1.
All inputs are finite; a program needn't handle non-finite values.
Results may differ from the reference program's by a relative error of at most 0.0018.
Values may be sent and summed in bfloat16 or wider, within the bound.
A program may use at most 64 MiB of HBM per device.

```python
import math
import jax
import jax.numpy as jnp
from jax import lax

CX = 128
CY = 16
CZ = 16
BOX = 4
ZONE = 256
NNZ = 5
GRID_POINTS_EAST = 512
GRID_POINTS_NORTH = 64
GRID_POINTS_UP = 32
BOXES = 512
NBLOCKS = 64
N_SEC = 4
N_BLK = 2
N_GY = 4


def draw_entry_target_tile(key, part):
    local_key = jax.random.fold_in(key, 11)
    rows_index = jnp.arange(NBLOCKS, dtype=jnp.int32)[:, None]
    offsets = jax.random.randint(local_key, (NBLOCKS, NNZ), 1, NBLOCKS, dtype=jnp.int32)
    columns = (rows_index + offsets) % NBLOCKS
    return columns.at[:, 0].set(rows_index[:, 0]).astype(jnp.int32)


def draw_nonempty_entries_per_strip(key, part):
    local_key = jax.random.fold_in(key, 23)
    counts = jax.random.randint(local_key, (NBLOCKS,), 1, NNZ + 1, dtype=jnp.int32)
    return counts.at[0].set(NNZ).at[1].set(1).astype(jnp.int32)


def level_of(own_key, shape, split, smallest, high):
    factor_of, own = 1.0, jax.random.fold_in(own_key, 6)
    for dim, blocks in split:
        heights = jnp.exp(jax.random.uniform(jax.random.fold_in(own, dim), (blocks,), jnp.float32, smallest / len(split), high / len(split)))
        factor_of = factor_of * jnp.repeat(heights, shape[dim] // blocks).reshape([-1 if axis == dim else 1 for axis in range(len(shape))])
    return factor_of


def gaussian(stream_key, shape, width, reach, shards=(), held_as=jnp.bfloat16):
    result = width * jax.random.normal(stream_key, shape, jnp.float32)
    if shards:
        result = result * level_of(stream_key, shape, shards, -0.22, 0.18)
    return jnp.clip(result, -reach, reach).astype(held_as)


def setup_inputs(seed: int = 0) -> dict:
    key_of = jax.random.split(jax.random.key(seed), 9)
    return {
        "normalized_kelvin": jnp.clip(0.6 + 1.4 * jax.random.uniform(key_of[0], (GRID_POINTS_UP, GRID_POINTS_NORTH, GRID_POINTS_EAST), jnp.float32) ** level_of(key_of[0], (GRID_POINTS_UP, GRID_POINTS_NORTH, GRID_POINTS_EAST), ((0, 2), (1, 4), (2, 4)), -0.2, 0.2), 0.6, 2.0),
        "co2_molar_part": jnp.clip(0.02 + 0.18 * jax.random.uniform(key_of[1], (GRID_POINTS_UP, GRID_POINTS_NORTH, GRID_POINTS_EAST), jnp.float32) ** level_of(key_of[1], (GRID_POINTS_UP, GRID_POINTS_NORTH, GRID_POINTS_EAST), ((0, 2), (1, 4), (2, 4)), -0.2, 0.2), 0.02, 0.2),
        "h2o_molar_part": jnp.clip(0.02 + 0.23 * jax.random.uniform(key_of[2], (GRID_POINTS_UP, GRID_POINTS_NORTH, GRID_POINTS_EAST), jnp.float32) ** level_of(key_of[2], (GRID_POINTS_UP, GRID_POINTS_NORTH, GRID_POINTS_EAST), ((0, 2), (1, 4), (2, 4)), -0.2, 0.2), 0.02, 0.25),
        "particulate_scaled": jnp.clip(jnp.exp(math.log(1.0) - 4.6051702 * jax.random.uniform(key_of[3], (GRID_POINTS_UP, GRID_POINTS_NORTH, GRID_POINTS_EAST), jnp.float32) ** level_of(key_of[3], (GRID_POINTS_UP, GRID_POINTS_NORTH, GRID_POINTS_EAST), ((0, 2), (1, 4), (2, 4)), -0.2, 0.2)), 0.01, 1.0),
        "region_local_subgrids": jax.vmap(lambda own: jax.random.permutation(own, BOXES))(jax.random.split(key_of[4], N_SEC * N_BLK * N_GY)).reshape((N_SEC, N_BLK, N_GY, BOXES)).astype(jnp.int32),
        "entry_target_tile": draw_entry_target_tile(jax.random.fold_in(key_of[8], 71), 0),
        "nonempty_entries_per_strip": draw_nonempty_entries_per_strip(jax.random.fold_in(key_of[8], 71), 0),
        "transfer_matrix_tiles": gaussian(key_of[7], (NBLOCKS, NNZ, ZONE, ZONE), (ZONE * NNZ) ** -0.5, 0.15625, ((0, 32),)),
    }


diffusion_rates = (0.12, 0.1, 0.1, 0.02)
vapour_attenuation_rate = (0.4, 1.6, 6.4, 25.6)
mixture_share_offset = (0.3, 0.25, 0.2, 0.15)
mixture_share_slope = (-0.05, 0.02, 0.03, 0.01)
particulate_attenuation_rate = 1.5
radiance_multiplier = 0.05
heating_rate = 0.1


def radiant_output_of_region(normalized_kelvin, co2_molar_part, h2o_molar_part, particulate_scaled):
    molecular_constituents = co2_molar_part + h2o_molar_part
    overall_summation = jnp.zeros_like(normalized_kelvin)
    for region_position in range(4):
        greybody_share = mixture_share_offset[region_position] + mixture_share_slope[region_position] * normalized_kelvin
        overall_summation = overall_summation + greybody_share * (vapour_attenuation_rate[region_position] * molecular_constituents + particulate_attenuation_rate * particulate_scaled * normalized_kelvin)
    kelvin_tesseract = normalized_kelvin * normalized_kelvin * normalized_kelvin * normalized_kelvin
    return radiance_multiplier * kelvin_tesseract * overall_summation


def to_boxes(whole):
    shaped = whole.reshape(N_BLK, CZ // BOX, BOX, N_GY, CY // BOX, BOX, N_SEC, CX // BOX, BOX)
    summed = jnp.sum(shaped, axis=(2, 5, 8)) * (1.0 / (BOX * BOX * BOX))
    return summed.transpose(4, 0, 2, 1, 3, 5).reshape(N_SEC, N_BLK, N_GY, BOXES)


def from_boxes(parts):
    shaped = parts.reshape(N_SEC, N_BLK, N_GY, CZ // BOX, 1, CY // BOX, 1, CX // BOX, 1)
    spread = jnp.broadcast_to(shaped, (N_SEC, N_BLK, N_GY, CZ // BOX, BOX, CY // BOX, BOX, CX // BOX, BOX))
    spread = spread.reshape(N_SEC, N_BLK, N_GY, CZ, CY, CX)
    return spread.transpose(1, 3, 2, 4, 0, 5).reshape(GRID_POINTS_UP, GRID_POINTS_NORTH, GRID_POINTS_EAST)


def row_product(items):
    matrix, picked_row = items
    return jnp.einsum("kij,kj->i", matrix.astype(jnp.float32), picked_row.astype(jnp.float32))


def reference(normalized_kelvin, co2_molar_part, h2o_molar_part, particulate_scaled, region_local_subgrids, entry_target_tile, nonempty_entries_per_strip, transfer_matrix_tiles):
    constituent_arrays = jnp.stack([normalized_kelvin, co2_molar_part, h2o_molar_part, particulate_scaled])
    padded = jnp.pad(constituent_arrays, ((0, 0), (1, 1), (1, 1), (1, 1)))
    beside = padded[:, 2:, 1:-1, 1:-1] + padded[:, :-2, 1:-1, 1:-1]
    beside = beside + padded[:, 1:-1, 2:, 1:-1] + padded[:, 1:-1, :-2, 1:-1]
    beside = beside + padded[:, 1:-1, 1:-1, 2:] + padded[:, 1:-1, 1:-1, :-2]
    rates = jnp.array(diffusion_rates, jnp.float32)[:, None, None, None]
    swept = constituent_arrays + rates * (beside - 6.0 * constituent_arrays)
    radiated_energy_rate = radiant_output_of_region(normalized_kelvin, co2_molar_part, h2o_molar_part, particulate_scaled)
    box_parts = to_boxes(radiated_energy_rate)
    zone_emission = jnp.take_along_axis(box_parts, region_local_subgrids, axis=3)
    emitted = zone_emission.astype(jnp.bfloat16).reshape(NBLOCKS, ZONE)
    picked = emitted[entry_target_tile]
    live_slots = jnp.arange(NNZ, dtype=jnp.int32)[None, :] < nonempty_entries_per_strip[:, None]
    picked = jnp.where(live_slots[:, :, None], picked, jnp.zeros_like(picked))
    taken_in_light = lax.map(row_product, (transfer_matrix_tiles, picked))
    net_zone = taken_in_light.reshape(N_SEC, N_BLK, N_GY, BOXES) - zone_emission
    first = jnp.arange(N_SEC, dtype=jnp.int32)[:, None, None, None]
    second = jnp.arange(N_BLK, dtype=jnp.int32)[None, :, None, None]
    third = jnp.arange(N_GY, dtype=jnp.int32)[None, None, :, None]
    box_net = jnp.zeros_like(net_zone).at[first, second, third, region_local_subgrids].set(net_zone)
    source = from_boxes(box_net)
    return (swept[0] + heating_rate * source, swept[1], swept[2], swept[3], source)
```

```python
import functools

import jax
import jax.numpy as jnp
from jax import lax
from jax.experimental import pallas as pl
from jax.experimental.pallas import tpu as pltpu
from jax.sharding import PartitionSpec as P

BOX = 4
AXES = ("sec", "blk", "gy")

diffusion_rates = (0.12, 0.1, 0.1, 0.02)
vapour_attenuation_rate = (0.4, 1.6, 6.4, 25.6)
mixture_share_offset = (0.3, 0.25, 0.2, 0.15)
mixture_share_slope = (-0.05, 0.02, 0.03, 0.01)
particulate_attenuation_rate = 1.5
radiance_multiplier = 0.05
heating_rate = 0.1

SHARE_OFFSET = sum(mixture_share_offset)
SHARE_SLOPE = sum(mixture_share_slope)
VAPOUR_OFFSET = sum(b * k for b, k in zip(mixture_share_offset, vapour_attenuation_rate))
VAPOUR_SLOPE = sum(c * k for c, k in zip(mixture_share_slope, vapour_attenuation_rate))

MESH = pl.DeviceIdType.MESH
NT = (((1,), (1,)), ((), ()))
TN = (((0,), (0,)), ((), ()))


def iota(shape, dim):
    return lax.broadcasted_iota(jnp.int32, shape, dim)


def group_sum(value, axis):
    size = value.shape[axis]
    place = iota(value.shape, axis)
    for step in (1, 2):
        above = pltpu.roll(value, size - step, axis)
        below = pltpu.roll(value, step, axis)
        value = value + jnp.where((place & step) == 0, above, below)
    return value


def kernel(
    dims,
    counts,
    kelvin_hbm,
    co2_hbm,
    h2o_hbm,
    soot_hbm,
    order_hbm,
    tile_ref,
    live_ref,
    matrix_hbm,
    *rest,
):
    outs = rest[:5]
    (
        fields,
        order_ref,
        matrix,
        done,
        gathered,
        z_out,
        y_out,
        x_out,
        z_in,
        y_in,
        x_in,
        in_sem,
        out_sem,
        face_send,
        face_recv,
        send_sem,
        recv_sem,
    ) = rest[5:]
    cz, cy, cx = dims
    n_sec, n_blk, n_gy = counts
    cells = cz * cy
    rows = matrix.shape[0]
    slots = matrix.shape[1]
    zones = order_ref.shape[1]
    zone = zones // rows
    n_plane = n_blk * n_gy
    sec, blk, gy = (lax.axis_index(a) for a in AXES)
    plane = blk * n_gy + gy
    me = sec * n_plane + plane

    copies = [
        pltpu.make_async_copy(src, fields.at[i], in_sem.at[i])
        for i, src in enumerate((kelvin_hbm, co2_hbm, h2o_hbm, soot_hbm))
    ]
    copies.append(pltpu.make_async_copy(order_hbm, order_ref, in_sem.at[4]))
    copies.append(pltpu.make_async_copy(matrix_hbm, matrix, in_sem.at[5]))
    for copy in copies:
        copy.start()

    def plane_peer(i):
        flat = lax.rem(plane + i, n_plane)
        return {"blk": lax.div(flat, n_gy), "gy": lax.rem(flat, n_gy)}

    def sec_peer(i):
        return {"sec": lax.rem(sec + i, n_sec)}

    def each(count, body):
        if count <= 32:
            for i in range(1, count):
                body(i)
        else:
            lax.fori_loop(1, count, lambda i, c: (body(i), c)[1], 0)

    barrier = pltpu.get_barrier_semaphore()
    for count, peer in ((n_plane, plane_peer), (n_sec, sec_peer)):
        each(
            count,
            lambda i, peer=peer: pl.semaphore_signal(
                barrier, inc=1, device_id=peer(i), device_id_type=MESH
            ),
        )

    places = (("sec", sec, n_sec), ("blk", blk, n_blk), ("gy", gy, n_gy))
    landing = (x_in, z_in, y_in)
    leaving = (x_out, z_out, y_out)
    for (_, at, size), land in zip(places, landing):
        for side, edge in ((0, 0), (1, size - 1)):

            @pl.when(at == edge)
            def _(land=land, side=side):
                land[side] = jnp.zeros(land.shape[1:], land.dtype)

    for copy in copies[:5]:
        copy.wait()

    kelvin = fields[0]
    vapour = fields[1] + fields[2]
    soot_kelvin = fields[3] * kelvin
    share = vapour * (VAPOUR_OFFSET + VAPOUR_SLOPE * kelvin) + (
        particulate_attenuation_rate * soot_kelvin * (SHARE_OFFSET + SHARE_SLOPE * kelvin)
    )
    squared = kelvin * kelvin
    emission = radiance_multiplier * (squared * squared) * share
    slabs = emission.reshape(cz // BOX, BOX, cy, cx)
    slabs = (slabs[:, 0] + slabs[:, 1] + slabs[:, 2] + slabs[:, 3]).reshape(cells // BOX, cx)
    box_mean = group_sum(group_sum(slabs, 0), 1) * (1.0 / (BOX * BOX * BOX))

    order = order_ref[...]
    across = cx // BOX
    x_shape = (cx, zones)
    r_shape = (cells // BOX, zones)
    x_at = iota(x_shape, 0)
    r_at = iota(r_shape, 0)
    same_x = lax.rem(order, across) == lax.div(x_at, BOX)
    box_row = lax.div(r_at, cy) * (cy // BOX) + lax.div(lax.rem(r_at, cy), BOX)
    same_r = lax.div(order, across) == box_row
    pick_x = jnp.where(same_x & (lax.rem(x_at, BOX) == 0), 1.0, 0.0).astype(jnp.bfloat16)
    pick_r = same_r & (lax.rem(r_at, BOX) == 0)
    by_row = jnp.dot(box_mean.astype(jnp.bfloat16), pick_x, preferred_element_type=jnp.float32)
    emitted = jnp.sum(jnp.where(pick_r, by_row, 0.0), axis=0, keepdims=True)
    for r in range(rows):
        gathered[me * rows + r] = emitted[:, r * zone : (r + 1) * zone]

    lane = iota((cells, cx), 1)
    packed = jnp.zeros((cells, cx), jnp.float32)
    for f in range(4):
        field = fields.at[f]
        z_out[0, f] = field[pl.ds(0, cy), :]
        z_out[1, f] = field[pl.ds(cells - cy, cy), :]
        y_out[0, f] = field[pl.ds(0, cz, stride=cy), :]
        y_out[1, f] = field[pl.ds(cy - 1, cz, stride=cy), :]
        packed = jnp.where((lane >> 1) == f, pltpu.roll(field[...], 2 * f + 1, 1), packed)
    x_out[...] = jnp.transpose(packed)[:8]

    pl.semaphore_wait(barrier, n_plane - 1 + n_sec - 1)

    def push(start, length, peer, stage):
        block = gathered.at[pl.ds(start, length)]
        pltpu.make_async_remote_copy(
            src_ref=block,
            dst_ref=block,
            send_sem=send_sem.at[stage],
            recv_sem=recv_sem.at[stage],
            device_id=peer,
            device_id_type=MESH,
        ).start()

    def settle(length, sem):
        block = gathered.at[pl.ds(0, length)]
        pltpu.make_async_copy(block, block, sem).wait()

    each(n_plane, lambda i: push(me * rows, rows, plane_peer(i), 0))

    def face(which, side):
        axis, at, _ = places[which]
        source = x_out if which == 0 else leaving[which].at[side]
        return pltpu.make_async_remote_copy(
            src_ref=source,
            dst_ref=landing[which].at[1 - side],
            send_sem=face_send.at[which, side],
            recv_sem=face_recv.at[which, 1 - side],
            device_id={axis: at + (2 * side - 1)},
            device_id_type=MESH,
        )

    def has(which, side):
        _, at, size = places[which]
        return at > 0 if side == 0 else at < size - 1

    for which in (1, 2, 0):
        for side in (0, 1):

            @pl.when(has(which, side))
            def _(which=which, side=side):
                face(which, side).start()

    place = iota((cells, cx), 0)
    y_place = lax.rem(place, cy)
    for f in range(4):
        value = fields[f]
        total = jnp.where(place >= cy, pltpu.roll(value, cy, 0), 0.0)
        total += jnp.where(place < cells - cy, pltpu.roll(value, cells - cy, 0), 0.0)
        total += jnp.where(y_place > 0, pltpu.roll(value, 1, 0), 0.0)
        total += jnp.where(y_place < cy - 1, pltpu.roll(value, cells - 1, 0), 0.0)
        total += jnp.where(lane > 0, pltpu.roll(value, 1, 1), 0.0)
        total += jnp.where(lane < cx - 1, pltpu.roll(value, cx - 1, 1), 0.0)
        done[f] = value + diffusion_rates[f] * (total - 6.0 * value)

    settle((n_plane - 1) * rows, recv_sem.at[0])
    each(n_sec, lambda i: push(sec * n_plane * rows, n_plane * rows, sec_peer(i), 1))

    for which in (0, 1, 2):
        for side in (0, 1):

            @pl.when(has(which, side))
            def _(which=which, side=side):
                face(which, 1 - side).wait_recv()

    shape = (16, 4 * cx)
    row, column = iota(shape, 0), iota(shape, 1)
    chosen = ((row < 8) & (column == (row >> 1) * cx) & ((row & 1) == 0)) | (
        (row >= 8) & (column == ((row - 8) >> 1) * cx + cx - 1) & ((row & 1) == 1)
    )
    sides = jnp.concatenate([x_in[0], x_in[1]], axis=0)
    x_add = lax.dot_general(
        sides,
        jnp.where(chosen, 1.0, 0.0),
        TN,
        precision=lax.Precision.HIGHEST,
        preferred_element_type=jnp.float32,
    )
    for f in (1, 2, 3, 0):
        rate = diffusion_rates[f]
        out = done.at[f]
        out[...] += rate * x_add[:, f * cx : (f + 1) * cx]
        out[pl.ds(0, cy), :] += rate * z_in[0, f]
        out[pl.ds(cells - cy, cy), :] += rate * z_in[1, f]
        out[pl.ds(0, cz, stride=cy), :] += rate * y_in[0, f]
        out[pl.ds(cy - 1, cz, stride=cy), :] += rate * y_in[1, f]
        if f:
            pltpu.make_async_copy(out, outs[f], out_sem.at[f]).start()

    spread_x = jnp.where(same_x, 1.0, 0.0).astype(jnp.bfloat16)
    copies[5].wait()
    settle((n_sec - 1) * n_plane * rows, recv_sem.at[1])

    absorbed = []
    for r in range(rows):
        total = jnp.zeros((1, zone), jnp.float32)
        for k in range(slots):
            tile = jnp.clip(tile_ref[r, k], 0, gathered.shape[0] - 1)
            picked = jnp.where(k < live_ref[r], gathered[tile], 0.0).astype(jnp.bfloat16)
            total += lax.dot_general(picked, matrix[r, k], NT, preferred_element_type=jnp.float32)
        absorbed.append(total)
    absorbed = jnp.concatenate(absorbed, axis=1)
    high = absorbed.astype(jnp.bfloat16).astype(jnp.float32)
    low = absorbed - high
    both = jnp.concatenate(
        [jnp.where(same_r, high, 0.0), jnp.where(same_r, low, 0.0)], axis=0
    ).astype(jnp.bfloat16)
    carried = lax.dot_general(both, spread_x, NT, preferred_element_type=jnp.float32)
    net = carried[: cells // BOX] + carried[cells // BOX :] - box_mean
    source = jnp.broadcast_to(
        net.reshape(cz // BOX, 1, cy, cx), (cz // BOX, BOX, cy, cx)
    ).reshape(cells, cx)
    done[4] = source
    done[0] += heating_rate * source
    for i in (4, 0):
        pltpu.make_async_copy(done.at[i], outs[i], out_sem.at[i]).start()

    settle((n_plane - 1) * rows, send_sem.at[0])
    settle((n_sec - 1) * n_plane * rows, send_sem.at[1])
    for which in (0, 1, 2):
        for side in (0, 1):

            @pl.when(has(which, side))
            def _(which=which, side=side):
                face(which, side).wait_send()

    for i in range(5):
        pltpu.make_async_copy(done.at[i], outs[i], out_sem.at[i]).wait()


def solution(mesh):
    counts = tuple(mesh.shape[a] for a in AXES)

    def local(kelvin, co2, h2o, soot, order, tiles, live, matrix):
        dims = kelvin.shape
        cz, cy, cx = dims
        cells = cz * cy
        rows = matrix.shape[0]
        zone = matrix.shape[2]
        blocks = counts[0] * counts[1] * counts[2] * rows
        flat = [a.reshape(cells, cx) for a in (kelvin, co2, h2o, soot)]
        order = order.reshape(1, -1)
        anywhere = pl.BlockSpec(memory_space=pl.ANY)
        scalars = pl.BlockSpec(memory_space=pltpu.SMEM)
        f32 = jnp.float32
        outs = pl.pallas_call(
            functools.partial(kernel, dims, counts),
            out_shape=[jax.ShapeDtypeStruct((cells, cx), f32)] * 5,
            in_specs=[anywhere] * 5 + [scalars] * 2 + [anywhere],
            out_specs=[anywhere] * 5,
            scratch_shapes=[
                pltpu.VMEM((4, cells, cx), f32),
                pltpu.VMEM(order.shape, jnp.int32),
                pltpu.VMEM(matrix.shape, matrix.dtype),
                pltpu.VMEM((5, cells, cx), f32),
                pltpu.VMEM((blocks, 1, zone), f32),
                pltpu.VMEM((2, 4, cy, cx), f32),
                pltpu.VMEM((2, 4, cz, cx), f32),
                pltpu.VMEM((8, cells), f32),
                pltpu.VMEM((2, 4, cy, cx), f32),
                pltpu.VMEM((2, 4, cz, cx), f32),
                pltpu.VMEM((2, 8, cells), f32),
                pltpu.SemaphoreType.DMA((6,)),
                pltpu.SemaphoreType.DMA((5,)),
                pltpu.SemaphoreType.DMA((3, 2)),
                pltpu.SemaphoreType.DMA((3, 2)),
                pltpu.SemaphoreType.DMA((2,)),
                pltpu.SemaphoreType.DMA((2,)),
            ],
            compiler_params=pltpu.CompilerParams(collective_id=0, has_side_effects=True),
        )(*flat, order, tiles, live, matrix)
        return tuple(o.reshape(dims) for o in outs)

    cell = P("blk", "gy", "sec")
    block = P(AXES)
    return jax.shard_map(
        local,
        mesh=mesh,
        in_specs=(cell,) * 4 + (P("sec", "blk", "gy", None), P(AXES, None), block, P(AXES, None, None, None)),
        out_specs=(cell,) * 5,
        check_vma=False,
    )
```

```python
import functools

import jax
import jax.numpy as jnp
from jax import lax
from jax.experimental import pallas as pl
from jax.experimental.pallas import tpu as pltpu
from jax.sharding import PartitionSpec as P

BOX = 4
AXES = ("sec", "blk", "gy")

diffusion_rates = (0.12, 0.1, 0.1, 0.02)
vapour_attenuation_rate = (0.4, 1.6, 6.4, 25.6)
mixture_share_offset = (0.3, 0.25, 0.2, 0.15)
mixture_share_slope = (-0.05, 0.02, 0.03, 0.01)
particulate_attenuation_rate = 1.5
radiance_multiplier = 0.05
heating_rate = 0.1

SHARE_OFFSET = sum(mixture_share_offset)
SHARE_SLOPE = sum(mixture_share_slope)
VAPOUR_OFFSET = sum(b * k for b, k in zip(mixture_share_offset, vapour_attenuation_rate))
VAPOUR_SLOPE = sum(c * k for c, k in zip(mixture_share_slope, vapour_attenuation_rate))

MESH = pl.DeviceIdType.MESH
NT = (((1,), (1,)), ((), ()))
TN = (((0,), (0,)), ((), ()))


def iota(shape, dim):
    return lax.broadcasted_iota(jnp.int32, shape, dim)


def group_sum(value, axis):
    size = value.shape[axis]
    place = iota(value.shape, axis)
    for step in (1, 2):
        above = pltpu.roll(value, size - step, axis)
        below = pltpu.roll(value, step, axis)
        value = value + jnp.where((place & step) == 0, above, below)
    return value


def kernel(
    dims,
    counts,
    kelvin_hbm,
    co2_hbm,
    h2o_hbm,
    soot_hbm,
    order_hbm,
    tile_ref,
    live_ref,
    matrix_hbm,
    *rest,
):
    done = rest[0]
    (
        fields,
        order_ref,
        matrix,
        gathered,
        z_out,
        y_out,
        x_out,
        z_in,
        y_in,
        x_in,
        in_sem,
        face_send,
        face_recv,
        send_sem,
        recv_sem,
    ) = rest[1:]
    cz, cy, cx = dims
    n_sec, n_blk, n_gy = counts
    cells = cz * cy
    rows = matrix.shape[0]
    slots = matrix.shape[1]
    zones = order_ref.shape[1]
    zone = zones // rows
    n_plane = n_blk * n_gy
    sec, blk, gy = (lax.axis_index(a) for a in AXES)
    plane = blk * n_gy + gy
    me = sec * n_plane + plane

    copies = [
        pltpu.make_async_copy(src, fields.at[i], in_sem.at[i])
        for i, src in enumerate((kelvin_hbm, co2_hbm, h2o_hbm, soot_hbm))
    ]
    copies.append(pltpu.make_async_copy(order_hbm, order_ref, in_sem.at[4]))
    copies.append(pltpu.make_async_copy(matrix_hbm, matrix, in_sem.at[5]))
    for copy in copies:
        copy.start()

    def plane_peer(i):
        flat = lax.rem(plane + i, n_plane)
        return {"blk": lax.div(flat, n_gy), "gy": lax.rem(flat, n_gy)}

    def sec_peer(i):
        return {"sec": lax.rem(sec + i, n_sec)}

    def each(count, body):
        if count <= 32:
            for i in range(1, count):
                body(i)
        else:
            lax.fori_loop(1, count, lambda i, c: (body(i), c)[1], 0)

    barrier = pltpu.get_barrier_semaphore()
    for count, peer in ((n_plane, plane_peer), (n_sec, sec_peer)):
        each(
            count,
            lambda i, peer=peer: pl.semaphore_signal(
                barrier, inc=1, device_id=peer(i), device_id_type=MESH
            ),
        )

    places = (("sec", sec, n_sec), ("blk", blk, n_blk), ("gy", gy, n_gy))
    landing = (x_in, z_in, y_in)
    leaving = (x_out, z_out, y_out)
    for (_, at, size), land in zip(places, landing):
        for side, edge in ((0, 0), (1, size - 1)):

            @pl.when(at == edge)
            def _(land=land, side=side):
                land[side] = jnp.zeros(land.shape[1:], land.dtype)

    for copy in copies[:5]:
        copy.wait()

    kelvin = fields[0]
    vapour = fields[1] + fields[2]
    soot_kelvin = fields[3] * kelvin
    share = vapour * (VAPOUR_OFFSET + VAPOUR_SLOPE * kelvin) + (
        particulate_attenuation_rate * soot_kelvin * (SHARE_OFFSET + SHARE_SLOPE * kelvin)
    )
    squared = kelvin * kelvin
    emission = radiance_multiplier * (squared * squared) * share
    slabs = emission.reshape(cz // BOX, BOX, cy, cx)
    slabs = (slabs[:, 0] + slabs[:, 1] + slabs[:, 2] + slabs[:, 3]).reshape(cells // BOX, cx)
    box_mean = group_sum(group_sum(slabs, 0), 1) * (1.0 / (BOX * BOX * BOX))

    order = order_ref[...]
    across = cx // BOX
    x_shape = (cx, zones)
    r_shape = (cells // BOX, zones)
    x_at = iota(x_shape, 0)
    r_at = iota(r_shape, 0)
    same_x = lax.rem(order, across) == lax.div(x_at, BOX)
    box_row = lax.div(r_at, cy) * (cy // BOX) + lax.div(lax.rem(r_at, cy), BOX)
    same_r = lax.div(order, across) == box_row
    pick_x = jnp.where(same_x & (lax.rem(x_at, BOX) == 0), 1.0, 0.0).astype(jnp.bfloat16)
    pick_r = same_r & (lax.rem(r_at, BOX) == 0)
    by_row = jnp.dot(box_mean.astype(jnp.bfloat16), pick_x, preferred_element_type=jnp.float32)
    emitted = jnp.sum(jnp.where(pick_r, by_row, 0.0), axis=0, keepdims=True)
    for r in range(rows):
        gathered[me * rows + r] = emitted[:, r * zone : (r + 1) * zone]

    lane = iota((cells, cx), 1)
    packed = jnp.zeros((cells, cx), jnp.float32)
    for f in range(4):
        field = fields.at[f]
        z_out[0, f] = field[pl.ds(0, cy), :]
        z_out[1, f] = field[pl.ds(cells - cy, cy), :]
        y_out[0, f] = field[pl.ds(0, cz, stride=cy), :]
        y_out[1, f] = field[pl.ds(cy - 1, cz, stride=cy), :]
        packed = jnp.where((lane >> 1) == f, pltpu.roll(field[...], 2 * f + 1, 1), packed)
    x_out[...] = jnp.transpose(packed)[:8]

    pl.semaphore_wait(barrier, n_plane - 1 + n_sec - 1)

    def push(start, length, peer, stage):
        block = gathered.at[pl.ds(start, length)]
        pltpu.make_async_remote_copy(
            src_ref=block,
            dst_ref=block,
            send_sem=send_sem.at[stage],
            recv_sem=recv_sem.at[stage],
            device_id=peer,
            device_id_type=MESH,
        ).start()

    def settle(length, sem):
        block = gathered.at[pl.ds(0, length)]
        pltpu.make_async_copy(block, block, sem).wait()

    each(n_plane, lambda i: push(me * rows, rows, plane_peer(i), 0))

    def face(which, side):
        axis, at, _ = places[which]
        source = x_out if which == 0 else leaving[which].at[side]
        return pltpu.make_async_remote_copy(
            src_ref=source,
            dst_ref=landing[which].at[1 - side],
            send_sem=face_send.at[which, side],
            recv_sem=face_recv.at[which, 1 - side],
            device_id={axis: at + (2 * side - 1)},
            device_id_type=MESH,
        )

    def has(which, side):
        _, at, size = places[which]
        return at > 0 if side == 0 else at < size - 1

    for which in (1, 2, 0):
        for side in (0, 1):

            @pl.when(has(which, side))
            def _(which=which, side=side):
                face(which, side).start()

    place = iota((cells, cx), 0)
    y_place = lax.rem(place, cy)
    for f in range(4):
        value = fields[f]
        total = jnp.where(place >= cy, pltpu.roll(value, cy, 0), 0.0)
        total += jnp.where(place < cells - cy, pltpu.roll(value, cells - cy, 0), 0.0)
        total += jnp.where(y_place > 0, pltpu.roll(value, 1, 0), 0.0)
        total += jnp.where(y_place < cy - 1, pltpu.roll(value, cells - 1, 0), 0.0)
        total += jnp.where(lane > 0, pltpu.roll(value, 1, 1), 0.0)
        total += jnp.where(lane < cx - 1, pltpu.roll(value, cx - 1, 1), 0.0)
        done[f] = value + diffusion_rates[f] * (total - 6.0 * value)

    settle((n_plane - 1) * rows, recv_sem.at[0])
    each(n_sec, lambda i: push(sec * n_plane * rows, n_plane * rows, sec_peer(i), 1))

    for which in (0, 1, 2):
        for side in (0, 1):

            @pl.when(has(which, side))
            def _(which=which, side=side):
                face(which, 1 - side).wait_recv()

    shape = (16, 4 * cx)
    row, column = iota(shape, 0), iota(shape, 1)
    chosen = ((row < 8) & (column == (row >> 1) * cx) & ((row & 1) == 0)) | (
        (row >= 8) & (column == ((row - 8) >> 1) * cx + cx - 1) & ((row & 1) == 1)
    )
    sides = jnp.concatenate([x_in[0], x_in[1]], axis=0)
    x_add = lax.dot_general(
        sides,
        jnp.where(chosen, 1.0, 0.0),
        TN,
        precision=lax.Precision.HIGHEST,
        preferred_element_type=jnp.float32,
    )
    for f in (1, 2, 3, 0):
        rate = diffusion_rates[f]
        out = done.at[f]
        out[...] += rate * x_add[:, f * cx : (f + 1) * cx]
        out[pl.ds(0, cy), :] += rate * z_in[0, f]
        out[pl.ds(cells - cy, cy), :] += rate * z_in[1, f]
        out[pl.ds(0, cz, stride=cy), :] += rate * y_in[0, f]
        out[pl.ds(cy - 1, cz, stride=cy), :] += rate * y_in[1, f]

    spread_x = jnp.where(same_x, 1.0, 0.0).astype(jnp.bfloat16)
    copies[5].wait()
    settle((n_sec - 1) * n_plane * rows, recv_sem.at[1])

    absorbed = []
    for r in range(rows):
        total = jnp.zeros((1, zone), jnp.float32)
        for k in range(slots):
            tile = jnp.clip(tile_ref[r, k], 0, gathered.shape[0] - 1)
            picked = jnp.where(k < live_ref[r], gathered[tile], 0.0).astype(jnp.bfloat16)
            total += lax.dot_general(picked, matrix[r, k], NT, preferred_element_type=jnp.float32)
        absorbed.append(total)
    absorbed = jnp.concatenate(absorbed, axis=1)
    high = absorbed.astype(jnp.bfloat16).astype(jnp.float32)
    low = absorbed - high
    both = jnp.concatenate(
        [jnp.where(same_r, high, 0.0), jnp.where(same_r, low, 0.0)], axis=0
    ).astype(jnp.bfloat16)
    carried = lax.dot_general(both, spread_x, NT, preferred_element_type=jnp.float32)
    net = carried[: cells // BOX] + carried[cells // BOX :] - box_mean
    source = jnp.broadcast_to(
        net.reshape(cz // BOX, 1, cy, cx), (cz // BOX, BOX, cy, cx)
    ).reshape(cells, cx)
    done[4] = source
    done[0] += heating_rate * source

    settle((n_plane - 1) * rows, send_sem.at[0])
    settle((n_sec - 1) * n_plane * rows, send_sem.at[1])
    for which in (0, 1, 2):
        for side in (0, 1):

            @pl.when(has(which, side))
            def _(which=which, side=side):
                face(which, side).wait_send()


def carry(source, *rest):
    outs, sem = rest[:5], rest[5]
    copies = [pltpu.make_async_copy(source.at[i], out, sem.at[i]) for i, out in enumerate(outs)]
    for copy in copies:
        copy.start()
    for copy in copies:
        copy.wait()


def solution(mesh):
    counts = tuple(mesh.shape[a] for a in AXES)

    def local(kelvin, co2, h2o, soot, order, tiles, live, matrix):
        dims = kelvin.shape
        cz, cy, cx = dims
        cells = cz * cy
        rows = matrix.shape[0]
        zone = matrix.shape[2]
        blocks = counts[0] * counts[1] * counts[2] * rows
        flat = [a.reshape(cells, cx) for a in (kelvin, co2, h2o, soot)]
        order = order.reshape(1, -1)
        anywhere = pl.BlockSpec(memory_space=pl.ANY)
        scalars = pl.BlockSpec(memory_space=pltpu.SMEM)
        f32 = jnp.float32
        done = pl.pallas_call(
            functools.partial(kernel, dims, counts),
            out_shape=jax.ShapeDtypeStruct((5, cells, cx), f32),
            in_specs=[anywhere] * 5 + [scalars] * 2 + [anywhere],
            out_specs=pl.BlockSpec(memory_space=pltpu.VMEM),
            scratch_shapes=[
                pltpu.VMEM((4, cells, cx), f32),
                pltpu.VMEM(order.shape, jnp.int32),
                pltpu.VMEM(matrix.shape, matrix.dtype),
                pltpu.VMEM((blocks, 1, zone), f32),
                pltpu.VMEM((2, 4, cy, cx), f32),
                pltpu.VMEM((2, 4, cz, cx), f32),
                pltpu.VMEM((8, cells), f32),
                pltpu.VMEM((2, 4, cy, cx), f32),
                pltpu.VMEM((2, 4, cz, cx), f32),
                pltpu.VMEM((2, 8, cells), f32),
                pltpu.SemaphoreType.DMA((6,)),
                pltpu.SemaphoreType.DMA((3, 2)),
                pltpu.SemaphoreType.DMA((3, 2)),
                pltpu.SemaphoreType.DMA((2,)),
                pltpu.SemaphoreType.DMA((2,)),
            ],
            compiler_params=pltpu.CompilerParams(collective_id=0, has_side_effects=True),
        )(*flat, order, tiles, live, matrix)
        outs = pl.pallas_call(
            carry,
            out_shape=[jax.ShapeDtypeStruct((cells, cx), f32)] * 5,
            in_specs=[anywhere],
            out_specs=[anywhere] * 5,
            scratch_shapes=[pltpu.SemaphoreType.DMA((5,))],
        )(done)
        return tuple(o.reshape(dims) for o in outs)

    cell = P("blk", "gy", "sec")
    block = P(AXES)
    return jax.shard_map(
        local,
        mesh=mesh,
        in_specs=(cell,) * 4 + (P("sec", "blk", "gy", None), P(AXES, None), block, P(AXES, None, None, None)),
        out_specs=(cell,) * 5,
        check_vma=False,
    )
```

```python
import functools

import jax
import jax.numpy as jnp
from jax import lax
from jax.experimental import pallas as pl
from jax.experimental.pallas import tpu as pltpu
from jax.sharding import PartitionSpec as P

BOX = 4
AXES = ("sec", "blk", "gy")

diffusion_rates = (0.12, 0.1, 0.1, 0.02)
vapour_attenuation_rate = (0.4, 1.6, 6.4, 25.6)
mixture_share_offset = (0.3, 0.25, 0.2, 0.15)
mixture_share_slope = (-0.05, 0.02, 0.03, 0.01)
particulate_attenuation_rate = 1.5
radiance_multiplier = 0.05
heating_rate = 0.1

SHARE_OFFSET = sum(mixture_share_offset)
SHARE_SLOPE = sum(mixture_share_slope)
VAPOUR_OFFSET = sum(b * k for b, k in zip(mixture_share_offset, vapour_attenuation_rate))
VAPOUR_SLOPE = sum(c * k for c, k in zip(mixture_share_slope, vapour_attenuation_rate))

MESH = pl.DeviceIdType.MESH
NT = (((1,), (1,)), ((), ()))
TN = (((0,), (0,)), ((), ()))


def iota(shape, dim):
    return lax.broadcasted_iota(jnp.int32, shape, dim)


def group_sum(value, axis):
    size = value.shape[axis]
    place = iota(value.shape, axis)
    for step in (1, 2):
        above = pltpu.roll(value, size - step, axis)
        below = pltpu.roll(value, step, axis)
        value = value + jnp.where((place & step) == 0, above, below)
    return value


def kernel(
    dims,
    counts,
    kelvin_hbm,
    co2_hbm,
    h2o_hbm,
    soot_hbm,
    order_hbm,
    tile_ref,
    live_ref,
    matrix_hbm,
    *rest,
):
    done = rest[0]
    (
        fields,
        order_ref,
        matrix,
        gathered,
        z_out,
        y_out,
        x_out,
        z_in,
        y_in,
        x_in,
        in_sem,
        face_send,
        face_recv,
        send_sem,
        recv_sem,
    ) = rest[1:]
    cz, cy, cx = dims
    n_sec, n_blk, n_gy = counts
    cells = cz * cy
    rows = matrix.shape[0]
    slots = matrix.shape[1]
    zones = order_ref.shape[1]
    zone = zones // rows
    n_plane = n_blk * n_gy
    sec, blk, gy = (lax.axis_index(a) for a in AXES)
    plane = blk * n_gy + gy
    me = sec * n_plane + plane
    n_all = n_sec * n_plane

    copies = [
        pltpu.make_async_copy(src, fields.at[i], in_sem.at[i])
        for i, src in enumerate((kelvin_hbm, co2_hbm, h2o_hbm, soot_hbm))
    ]
    copies.append(pltpu.make_async_copy(order_hbm, order_ref, in_sem.at[4]))
    copies.append(pltpu.make_async_copy(matrix_hbm, matrix, in_sem.at[5]))
    for copy in copies:
        copy.start()

    def plane_peer(i):
        flat = lax.rem(me + i, n_all)
        return {
            "sec": lax.div(flat, n_plane),
            "blk": lax.rem(lax.div(flat, n_gy), n_blk),
            "gy": lax.rem(flat, n_gy),
        }

    def each(count, body):
        if count <= 32:
            for i in range(1, count):
                body(i)
        else:
            lax.fori_loop(1, count, lambda i, c: (body(i), c)[1], 0)

    barrier = pltpu.get_barrier_semaphore()
    each(
        n_all,
        lambda i: pl.semaphore_signal(
            barrier, inc=1, device_id=plane_peer(i), device_id_type=MESH
        ),
    )

    places = (("sec", sec, n_sec), ("blk", blk, n_blk), ("gy", gy, n_gy))
    landing = (x_in, z_in, y_in)
    leaving = (x_out, z_out, y_out)
    for (_, at, size), land in zip(places, landing):
        for side, edge in ((0, 0), (1, size - 1)):

            @pl.when(at == edge)
            def _(land=land, side=side):
                land[side] = jnp.zeros(land.shape[1:], land.dtype)

    for copy in copies[:5]:
        copy.wait()

    kelvin = fields[0]
    vapour = fields[1] + fields[2]
    soot_kelvin = fields[3] * kelvin
    share = vapour * (VAPOUR_OFFSET + VAPOUR_SLOPE * kelvin) + (
        particulate_attenuation_rate * soot_kelvin * (SHARE_OFFSET + SHARE_SLOPE * kelvin)
    )
    squared = kelvin * kelvin
    emission = radiance_multiplier * (squared * squared) * share
    slabs = emission.reshape(cz // BOX, BOX, cy, cx)
    slabs = (slabs[:, 0] + slabs[:, 1] + slabs[:, 2] + slabs[:, 3]).reshape(cells // BOX, cx)
    box_mean = group_sum(group_sum(slabs, 0), 1) * (1.0 / (BOX * BOX * BOX))

    order = order_ref[...]
    across = cx // BOX
    x_shape = (cx, zones)
    r_shape = (cells // BOX, zones)
    x_at = iota(x_shape, 0)
    r_at = iota(r_shape, 0)
    same_x = lax.rem(order, across) == lax.div(x_at, BOX)
    box_row = lax.div(r_at, cy) * (cy // BOX) + lax.div(lax.rem(r_at, cy), BOX)
    same_r = lax.div(order, across) == box_row
    pick_x = jnp.where(same_x & (lax.rem(x_at, BOX) == 0), 1.0, 0.0).astype(jnp.bfloat16)
    pick_r = same_r & (lax.rem(r_at, BOX) == 0)
    by_row = jnp.dot(box_mean.astype(jnp.bfloat16), pick_x, preferred_element_type=jnp.float32)
    emitted = jnp.sum(jnp.where(pick_r, by_row, 0.0), axis=0, keepdims=True)
    for r in range(rows):
        gathered[me * rows + r] = emitted[:, r * zone : (r + 1) * zone]

    lane = iota((cells, cx), 1)
    packed = jnp.zeros((cells, cx), jnp.float32)
    for f in range(4):
        field = fields.at[f]
        z_out[0, f] = field[pl.ds(0, cy), :]
        z_out[1, f] = field[pl.ds(cells - cy, cy), :]
        y_out[0, f] = field[pl.ds(0, cz, stride=cy), :]
        y_out[1, f] = field[pl.ds(cy - 1, cz, stride=cy), :]
        packed = jnp.where((lane >> 1) == f, pltpu.roll(field[...], 2 * f + 1, 1), packed)
    x_out[...] = jnp.transpose(packed)[:8]

    pl.semaphore_wait(barrier, n_all - 1)

    def push(start, length, peer, stage):
        block = gathered.at[pl.ds(start, length)]
        pltpu.make_async_remote_copy(
            src_ref=block,
            dst_ref=block,
            send_sem=send_sem.at[stage],
            recv_sem=recv_sem.at[stage],
            device_id=peer,
            device_id_type=MESH,
        ).start()

    def settle(length, sem):
        block = gathered.at[pl.ds(0, length)]
        pltpu.make_async_copy(block, block, sem).wait()

    each(n_all, lambda i: push(me * rows, rows, plane_peer(i), 0))

    def face(which, side):
        axis, at, _ = places[which]
        source = x_out if which == 0 else leaving[which].at[side]
        return pltpu.make_async_remote_copy(
            src_ref=source,
            dst_ref=landing[which].at[1 - side],
            send_sem=face_send.at[which, side],
            recv_sem=face_recv.at[which, 1 - side],
            device_id={axis: at + (2 * side - 1)},
            device_id_type=MESH,
        )

    def has(which, side):
        _, at, size = places[which]
        return at > 0 if side == 0 else at < size - 1

    for which in (1, 2, 0):
        for side in (0, 1):

            @pl.when(has(which, side))
            def _(which=which, side=side):
                face(which, side).start()

    place = iota((cells, cx), 0)
    y_place = lax.rem(place, cy)
    for f in range(4):
        value = fields[f]
        total = jnp.where(place >= cy, pltpu.roll(value, cy, 0), 0.0)
        total += jnp.where(place < cells - cy, pltpu.roll(value, cells - cy, 0), 0.0)
        total += jnp.where(y_place > 0, pltpu.roll(value, 1, 0), 0.0)
        total += jnp.where(y_place < cy - 1, pltpu.roll(value, cells - 1, 0), 0.0)
        total += jnp.where(lane > 0, pltpu.roll(value, 1, 1), 0.0)
        total += jnp.where(lane < cx - 1, pltpu.roll(value, cx - 1, 1), 0.0)
        done[f] = value + diffusion_rates[f] * (total - 6.0 * value)

    for which in (0, 1, 2):
        for side in (0, 1):

            @pl.when(has(which, side))
            def _(which=which, side=side):
                face(which, 1 - side).wait_recv()

    shape = (16, 4 * cx)
    row, column = iota(shape, 0), iota(shape, 1)
    chosen = ((row < 8) & (column == (row >> 1) * cx) & ((row & 1) == 0)) | (
        (row >= 8) & (column == ((row - 8) >> 1) * cx + cx - 1) & ((row & 1) == 1)
    )
    sides = jnp.concatenate([x_in[0], x_in[1]], axis=0)
    x_add = lax.dot_general(
        sides,
        jnp.where(chosen, 1.0, 0.0),
        TN,
        precision=lax.Precision.HIGHEST,
        preferred_element_type=jnp.float32,
    )
    for f in (1, 2, 3, 0):
        rate = diffusion_rates[f]
        out = done.at[f]
        out[...] += rate * x_add[:, f * cx : (f + 1) * cx]
        out[pl.ds(0, cy), :] += rate * z_in[0, f]
        out[pl.ds(cells - cy, cy), :] += rate * z_in[1, f]
        out[pl.ds(0, cz, stride=cy), :] += rate * y_in[0, f]
        out[pl.ds(cy - 1, cz, stride=cy), :] += rate * y_in[1, f]

    spread_x = jnp.where(same_x, 1.0, 0.0).astype(jnp.bfloat16)
    copies[5].wait()
    settle((n_all - 1) * rows, recv_sem.at[0])

    absorbed = []
    for r in range(rows):
        total = jnp.zeros((1, zone), jnp.float32)
        for k in range(slots):
            tile = jnp.clip(tile_ref[r, k], 0, gathered.shape[0] - 1)
            picked = jnp.where(k < live_ref[r], gathered[tile], 0.0).astype(jnp.bfloat16)
            total += lax.dot_general(picked, matrix[r, k], NT, preferred_element_type=jnp.float32)
        absorbed.append(total)
    absorbed = jnp.concatenate(absorbed, axis=1)
    high = absorbed.astype(jnp.bfloat16).astype(jnp.float32)
    low = absorbed - high
    both = jnp.concatenate(
        [jnp.where(same_r, high, 0.0), jnp.where(same_r, low, 0.0)], axis=0
    ).astype(jnp.bfloat16)
    carried = lax.dot_general(both, spread_x, NT, preferred_element_type=jnp.float32)
    net = carried[: cells // BOX] + carried[cells // BOX :] - box_mean
    source = jnp.broadcast_to(
        net.reshape(cz // BOX, 1, cy, cx), (cz // BOX, BOX, cy, cx)
    ).reshape(cells, cx)
    done[4] = source
    done[0] += heating_rate * source

    settle((n_all - 1) * rows, send_sem.at[0])
    for which in (0, 1, 2):
        for side in (0, 1):

            @pl.when(has(which, side))
            def _(which=which, side=side):
                face(which, side).wait_send()


def carry(source, *rest):
    outs, held, in_sem, out_sem = rest[:5], *rest[5:]
    copies_in = [
        pltpu.make_async_copy(source.at[i], held.at[i], in_sem.at[i]) for i in range(len(outs))
    ]
    copies_out = [
        pltpu.make_async_copy(held.at[i], out, out_sem.at[i]) for i, out in enumerate(outs)
    ]
    for copy in copies_in:
        copy.start()
    for copy, onward in zip(copies_in, copies_out):
        copy.wait()
        onward.start()
    for copy in copies_out:
        copy.wait()


def solution(mesh):
    counts = tuple(mesh.shape[a] for a in AXES)

    def local(kelvin, co2, h2o, soot, order, tiles, live, matrix):
        dims = kelvin.shape
        cz, cy, cx = dims
        cells = cz * cy
        rows = matrix.shape[0]
        zone = matrix.shape[2]
        blocks = counts[0] * counts[1] * counts[2] * rows
        flat = [a.reshape(cells, cx) for a in (kelvin, co2, h2o, soot)]
        order = order.reshape(1, -1)
        anywhere = pl.BlockSpec(memory_space=pl.ANY)
        scalars = pl.BlockSpec(memory_space=pltpu.SMEM)
        f32 = jnp.float32
        done = pl.pallas_call(
            functools.partial(kernel, dims, counts),
            out_shape=jax.ShapeDtypeStruct((5, cells, cx), f32),
            in_specs=[anywhere] * 5 + [scalars] * 2 + [anywhere],
            out_specs=pl.BlockSpec(memory_space=pltpu.VMEM),
            scratch_shapes=[
                pltpu.VMEM((4, cells, cx), f32),
                pltpu.VMEM(order.shape, jnp.int32),
                pltpu.VMEM(matrix.shape, matrix.dtype),
                pltpu.VMEM((blocks, 1, zone), f32),
                pltpu.VMEM((2, 4, cy, cx), f32),
                pltpu.VMEM((2, 4, cz, cx), f32),
                pltpu.VMEM((8, cells), f32),
                pltpu.VMEM((2, 4, cy, cx), f32),
                pltpu.VMEM((2, 4, cz, cx), f32),
                pltpu.VMEM((2, 8, cells), f32),
                pltpu.SemaphoreType.DMA((6,)),
                pltpu.SemaphoreType.DMA((3, 2)),
                pltpu.SemaphoreType.DMA((3, 2)),
                pltpu.SemaphoreType.DMA((2,)),
                pltpu.SemaphoreType.DMA((2,)),
            ],
            compiler_params=pltpu.CompilerParams(collective_id=0, has_side_effects=True),
        )(*flat, order, tiles, live, matrix)
        outs = pl.pallas_call(
            carry,
            out_shape=[jax.ShapeDtypeStruct((cells, cx), f32)] * 5,
            in_specs=[anywhere],
            out_specs=[anywhere] * 5,
            scratch_shapes=[
                pltpu.VMEM((5, cells, cx), f32),
                pltpu.SemaphoreType.DMA((5,)),
                pltpu.SemaphoreType.DMA((5,)),
            ],
        )(done)
        return tuple(o.reshape(dims) for o in outs)

    cell = P("blk", "gy", "sec")
    block = P(AXES)
    return jax.shard_map(
        local,
        mesh=mesh,
        in_specs=(cell,) * 4 + (P("sec", "blk", "gy", None), P(AXES, None), block, P(AXES, None, None, None)),
        out_specs=(cell,) * 5,
        check_vma=False,
    )
```

```python
import functools

import jax
import jax.numpy as jnp
from jax import lax
from jax.experimental import pallas as pl
from jax.experimental.pallas import tpu as pltpu
from jax.sharding import PartitionSpec as P

BOX = 4
AXES = ("sec", "blk", "gy")

diffusion_rates = (0.12, 0.1, 0.1, 0.02)
vapour_attenuation_rate = (0.4, 1.6, 6.4, 25.6)
mixture_share_offset = (0.3, 0.25, 0.2, 0.15)
mixture_share_slope = (-0.05, 0.02, 0.03, 0.01)
particulate_attenuation_rate = 1.5
radiance_multiplier = 0.05
heating_rate = 0.1

SHARE_OFFSET = sum(mixture_share_offset)
SHARE_SLOPE = sum(mixture_share_slope)
VAPOUR_OFFSET = sum(b * k for b, k in zip(mixture_share_offset, vapour_attenuation_rate))
VAPOUR_SLOPE = sum(c * k for c, k in zip(mixture_share_slope, vapour_attenuation_rate))

MESH = pl.DeviceIdType.MESH
NT = (((1,), (1,)), ((), ()))
TN = (((0,), (0,)), ((), ()))


def iota(shape, dim):
    return lax.broadcasted_iota(jnp.int32, shape, dim)


def group_sum(value, axis):
    size = value.shape[axis]
    place = iota(value.shape, axis)
    for step in (1, 2):
        above = pltpu.roll(value, size - step, axis)
        below = pltpu.roll(value, step, axis)
        value = value + jnp.where((place & step) == 0, above, below)
    return value


def kernel(
    dims,
    counts,
    kelvin_hbm,
    co2_hbm,
    h2o_hbm,
    soot_hbm,
    order_hbm,
    tile_hbm,
    live_hbm,
    matrix_hbm,
    *rest,
):
    done = rest[0]
    (
        fields,
        order_ref,
        matrix,
        gathered,
        z_out,
        y_out,
        x_out,
        z_in,
        y_in,
        x_in,
        tile_ref,
        live_ref,
        in_sem,
        face_send,
        face_recv,
        send_sem,
        recv_sem,
    ) = rest[1:]
    cz, cy, cx = dims
    n_sec, n_blk, n_gy = counts
    cells = cz * cy
    rows = matrix.shape[0]
    slots = matrix.shape[1]
    zones = order_ref.shape[1]
    zone = zones // rows
    n_plane = n_blk * n_gy
    sec, blk, gy = (lax.axis_index(a) for a in AXES)
    plane = blk * n_gy + gy
    me = sec * n_plane + plane
    n_all = n_sec * n_plane

    copies = [
        pltpu.make_async_copy(src, fields.at[i], in_sem.at[i])
        for i, src in enumerate((kelvin_hbm, co2_hbm, h2o_hbm, soot_hbm))
    ]
    copies.append(pltpu.make_async_copy(order_hbm, order_ref, in_sem.at[4]))
    copies.append(pltpu.make_async_copy(matrix_hbm, matrix, in_sem.at[5]))
    copies.append(pltpu.make_async_copy(tile_hbm, tile_ref, in_sem.at[6]))
    copies.append(pltpu.make_async_copy(live_hbm, live_ref, in_sem.at[7]))
    for copy in copies:
        copy.start()

    def plane_peer(i):
        flat = lax.rem(me + i, n_all)
        return {
            "sec": lax.div(flat, n_plane),
            "blk": lax.rem(lax.div(flat, n_gy), n_blk),
            "gy": lax.rem(flat, n_gy),
        }

    def each(count, body):
        if count <= 32:
            for i in range(1, count):
                body(i)
        else:
            lax.fori_loop(1, count, lambda i, c: (body(i), c)[1], 0)

    barrier = pltpu.get_barrier_semaphore()
    each(
        n_all,
        lambda i: pl.semaphore_signal(
            barrier, inc=1, device_id=plane_peer(i), device_id_type=MESH
        ),
    )

    places = (("sec", sec, n_sec), ("blk", blk, n_blk), ("gy", gy, n_gy))
    landing = (x_in, z_in, y_in)
    leaving = (x_out, z_out, y_out)
    for (_, at, size), land in zip(places, landing):
        for side, edge in ((0, 0), (1, size - 1)):

            @pl.when(at == edge)
            def _(land=land, side=side):
                land[side] = jnp.zeros(land.shape[1:], land.dtype)

    for copy in copies[:5]:
        copy.wait()

    kelvin = fields[0]
    vapour = fields[1] + fields[2]
    soot_kelvin = fields[3] * kelvin
    share = vapour * (VAPOUR_OFFSET + VAPOUR_SLOPE * kelvin) + (
        particulate_attenuation_rate * soot_kelvin * (SHARE_OFFSET + SHARE_SLOPE * kelvin)
    )
    squared = kelvin * kelvin
    emission = radiance_multiplier * (squared * squared) * share
    slabs = emission.reshape(cz // BOX, BOX, cy, cx)
    slabs = (slabs[:, 0] + slabs[:, 1] + slabs[:, 2] + slabs[:, 3]).reshape(cells // BOX, cx)
    box_mean = group_sum(group_sum(slabs, 0), 1) * (1.0 / (BOX * BOX * BOX))

    order = order_ref[...]
    across = cx // BOX
    x_shape = (cx, zones)
    r_shape = (cells // BOX, zones)
    x_at = iota(x_shape, 0)
    r_at = iota(r_shape, 0)
    same_x = lax.rem(order, across) == lax.div(x_at, BOX)
    box_row = lax.div(r_at, cy) * (cy // BOX) + lax.div(lax.rem(r_at, cy), BOX)
    same_r = lax.div(order, across) == box_row
    pick_x = jnp.where(same_x & (lax.rem(x_at, BOX) == 0), 1.0, 0.0).astype(jnp.bfloat16)
    pick_r = same_r & (lax.rem(r_at, BOX) == 0)
    by_row = jnp.dot(box_mean.astype(jnp.bfloat16), pick_x, preferred_element_type=jnp.float32)
    emitted = jnp.sum(jnp.where(pick_r, by_row, 0.0), axis=0, keepdims=True)
    for r in range(rows):
        gathered[me * rows + r] = emitted[:, r * zone : (r + 1) * zone]

    lane = iota((cells, cx), 1)
    packed = jnp.zeros((cells, cx), jnp.float32)
    for f in range(4):
        field = fields.at[f]
        z_out[0, f] = field[pl.ds(0, cy), :]
        z_out[1, f] = field[pl.ds(cells - cy, cy), :]
        y_out[0, f] = field[pl.ds(0, cz, stride=cy), :]
        y_out[1, f] = field[pl.ds(cy - 1, cz, stride=cy), :]
        packed = jnp.where((lane >> 1) == f, pltpu.roll(field[...], 2 * f + 1, 1), packed)
    x_out[...] = jnp.transpose(packed)[:8]

    pl.semaphore_wait(barrier, n_all - 1)

    def push(start, length, peer, stage):
        block = gathered.at[pl.ds(start, length)]
        pltpu.make_async_remote_copy(
            src_ref=block,
            dst_ref=block,
            send_sem=send_sem.at[stage],
            recv_sem=recv_sem.at[stage],
            device_id=peer,
            device_id_type=MESH,
        ).start()

    def settle(length, sem):
        block = gathered.at[pl.ds(0, length)]
        pltpu.make_async_copy(block, block, sem).wait()

    each(n_all, lambda i: push(me * rows, rows, plane_peer(i), 0))

    def face(which, side):
        axis, at, _ = places[which]
        source = x_out if which == 0 else leaving[which].at[side]
        return pltpu.make_async_remote_copy(
            src_ref=source,
            dst_ref=landing[which].at[1 - side],
            send_sem=face_send.at[which, side],
            recv_sem=face_recv.at[which, 1 - side],
            device_id={axis: at + (2 * side - 1)},
            device_id_type=MESH,
        )

    def has(which, side):
        _, at, size = places[which]
        return at > 0 if side == 0 else at < size - 1

    for which in (1, 2, 0):
        for side in (0, 1):

            @pl.when(has(which, side))
            def _(which=which, side=side):
                face(which, side).start()

    place = iota((cells, cx), 0)
    y_place = lax.rem(place, cy)
    for f in range(4):
        value = fields[f]
        total = jnp.where(place >= cy, pltpu.roll(value, cy, 0), 0.0)
        total += jnp.where(place < cells - cy, pltpu.roll(value, cells - cy, 0), 0.0)
        total += jnp.where(y_place > 0, pltpu.roll(value, 1, 0), 0.0)
        total += jnp.where(y_place < cy - 1, pltpu.roll(value, cells - 1, 0), 0.0)
        total += jnp.where(lane > 0, pltpu.roll(value, 1, 1), 0.0)
        total += jnp.where(lane < cx - 1, pltpu.roll(value, cx - 1, 1), 0.0)
        done[f] = value + diffusion_rates[f] * (total - 6.0 * value)

    for which in (0, 1, 2):
        for side in (0, 1):

            @pl.when(has(which, side))
            def _(which=which, side=side):
                face(which, 1 - side).wait_recv()

    shape = (16, 4 * cx)
    row, column = iota(shape, 0), iota(shape, 1)
    chosen = ((row < 8) & (column == (row >> 1) * cx) & ((row & 1) == 0)) | (
        (row >= 8) & (column == ((row - 8) >> 1) * cx + cx - 1) & ((row & 1) == 1)
    )
    sides = jnp.concatenate([x_in[0], x_in[1]], axis=0)
    x_add = lax.dot_general(
        sides,
        jnp.where(chosen, 1.0, 0.0),
        TN,
        precision=lax.Precision.HIGHEST,
        preferred_element_type=jnp.float32,
    )
    for f in (1, 2, 3, 0):
        rate = diffusion_rates[f]
        out = done.at[f]
        out[...] += rate * x_add[:, f * cx : (f + 1) * cx]
        out[pl.ds(0, cy), :] += rate * z_in[0, f]
        out[pl.ds(cells - cy, cy), :] += rate * z_in[1, f]
        out[pl.ds(0, cz, stride=cy), :] += rate * y_in[0, f]
        out[pl.ds(cy - 1, cz, stride=cy), :] += rate * y_in[1, f]

    spread_x = jnp.where(same_x, 1.0, 0.0).astype(jnp.bfloat16)
    for copy in copies[5:]:
        copy.wait()
    settle((n_all - 1) * rows, recv_sem.at[0])

    absorbed = []
    for r in range(rows):
        total = jnp.zeros((1, zone), jnp.float32)
        for k in range(slots):
            tile = jnp.clip(tile_ref[r, k], 0, gathered.shape[0] - 1)
            picked = jnp.where(k < live_ref[r], gathered[tile], 0.0).astype(jnp.bfloat16)
            total += lax.dot_general(picked, matrix[r, k], NT, preferred_element_type=jnp.float32)
        absorbed.append(total)
    absorbed = jnp.concatenate(absorbed, axis=1)
    high = absorbed.astype(jnp.bfloat16).astype(jnp.float32)
    low = absorbed - high
    both = jnp.concatenate(
        [jnp.where(same_r, high, 0.0), jnp.where(same_r, low, 0.0)], axis=0
    ).astype(jnp.bfloat16)
    carried = lax.dot_general(both, spread_x, NT, preferred_element_type=jnp.float32)
    net = carried[: cells // BOX] + carried[cells // BOX :] - box_mean
    source = jnp.broadcast_to(
        net.reshape(cz // BOX, 1, cy, cx), (cz // BOX, BOX, cy, cx)
    ).reshape(cells, cx)
    done[4] = source
    done[0] += heating_rate * source

    settle((n_all - 1) * rows, send_sem.at[0])
    for which in (0, 1, 2):
        for side in (0, 1):

            @pl.when(has(which, side))
            def _(which=which, side=side):
                face(which, side).wait_send()


def carry(source, *rest):
    outs, sem = rest[:5], rest[5]
    copies = [pltpu.make_async_copy(source.at[i], out, sem.at[i]) for i, out in enumerate(outs)]
    for copy in copies:
        copy.start()
    for copy in copies:
        copy.wait()


def solution(mesh):
    counts = tuple(mesh.shape[a] for a in AXES)

    def local(kelvin, co2, h2o, soot, order, tiles, live, matrix):
        dims = kelvin.shape
        cz, cy, cx = dims
        cells = cz * cy
        rows = matrix.shape[0]
        zone = matrix.shape[2]
        blocks = counts[0] * counts[1] * counts[2] * rows
        flat = [a.reshape(cells, cx) for a in (kelvin, co2, h2o, soot)]
        order = order.reshape(1, -1)
        anywhere = pl.BlockSpec(memory_space=pl.ANY)
        f32 = jnp.float32
        done = pl.pallas_call(
            functools.partial(kernel, dims, counts),
            out_shape=pltpu.VMEM((5, cells, cx), f32),
            in_specs=[anywhere] * 8,
            out_specs=pl.BlockSpec(memory_space=pltpu.VMEM),
            scratch_shapes=[
                pltpu.VMEM((4, cells, cx), f32),
                pltpu.VMEM(order.shape, jnp.int32),
                pltpu.VMEM(matrix.shape, matrix.dtype),
                pltpu.VMEM((blocks, 1, zone), f32),
                pltpu.VMEM((2, 4, cy, cx), f32),
                pltpu.VMEM((2, 4, cz, cx), f32),
                pltpu.VMEM((8, cells), f32),
                pltpu.VMEM((2, 4, cy, cx), f32),
                pltpu.VMEM((2, 4, cz, cx), f32),
                pltpu.VMEM((2, 8, cells), f32),
                pltpu.SMEM(tiles.shape, tiles.dtype),
                pltpu.SMEM(live.shape, live.dtype),
                pltpu.SemaphoreType.DMA((8,)),
                pltpu.SemaphoreType.DMA((3, 2)),
                pltpu.SemaphoreType.DMA((3, 2)),
                pltpu.SemaphoreType.DMA((2,)),
                pltpu.SemaphoreType.DMA((2,)),
            ],
            compiler_params=pltpu.CompilerParams(collective_id=0, has_side_effects=True),
        )(*flat, order, tiles, live, matrix)
        outs = pl.pallas_call(
            carry,
            out_shape=[jax.ShapeDtypeStruct((cells, cx), f32)] * 5,
            in_specs=[anywhere],
            out_specs=[anywhere] * 5,
            scratch_shapes=[
                pltpu.SemaphoreType.DMA((5,)),
            ],
            compiler_params=pltpu.CompilerParams(vmem_limit_bytes=4 << 20),
        )(done)
        return tuple(o.reshape(dims) for o in outs)

    cell = P("blk", "gy", "sec")
    block = P(AXES)
    return jax.shard_map(
        local,
        mesh=mesh,
        in_specs=(cell,) * 4 + (P("sec", "blk", "gy", None), P(AXES, None), block, P(AXES, None, None, None)),
        out_specs=(cell,) * 5,
        check_vma=False,
    )
```

```python
import functools

import jax
import jax.numpy as jnp
from jax import lax
from jax.experimental import pallas as pl
from jax.experimental.pallas import tpu as pltpu
from jax.sharding import PartitionSpec as P

BOX = 4
AXES = ("sec", "blk", "gy")

diffusion_rates = (0.12, 0.1, 0.1, 0.02)
vapour_attenuation_rate = (0.4, 1.6, 6.4, 25.6)
mixture_share_offset = (0.3, 0.25, 0.2, 0.15)
mixture_share_slope = (-0.05, 0.02, 0.03, 0.01)
particulate_attenuation_rate = 1.5
radiance_multiplier = 0.05
heating_rate = 0.1

SHARE_OFFSET = sum(mixture_share_offset)
SHARE_SLOPE = sum(mixture_share_slope)
VAPOUR_OFFSET = sum(b * k for b, k in zip(mixture_share_offset, vapour_attenuation_rate))
VAPOUR_SLOPE = sum(c * k for c, k in zip(mixture_share_slope, vapour_attenuation_rate))

MESH = pl.DeviceIdType.MESH
NT = (((1,), (1,)), ((), ()))
TN = (((0,), (0,)), ((), ()))


def iota(shape, dim):
    return lax.broadcasted_iota(jnp.int32, shape, dim)


def group_sum(value, axis):
    size = value.shape[axis]
    place = iota(value.shape, axis)
    for step in (1, 2):
        above = pltpu.roll(value, size - step, axis)
        below = pltpu.roll(value, step, axis)
        value = value + jnp.where((place & step) == 0, above, below)
    return value


def kernel(
    dims,
    counts,
    kelvin_hbm,
    co2_hbm,
    h2o_hbm,
    soot_hbm,
    order_hbm,
    tile_hbm,
    live_hbm,
    matrix_hbm,
    *rest,
):
    done = rest[0]
    (
        fields,
        order_ref,
        matrix,
        gathered,
        z_out,
        y_out,
        x_out,
        z_in,
        y_in,
        x_in,
        tile_ref,
        live_ref,
        in_sem,
        face_send,
        face_recv,
        send_sem,
        recv_sem,
    ) = rest[1:]
    cz, cy, cx = dims
    n_sec, n_blk, n_gy = counts
    cells = cz * cy
    rows = matrix.shape[0]
    slots = matrix.shape[1]
    zones = order_ref.shape[1]
    zone = zones // rows
    n_plane = n_blk * n_gy
    sec, blk, gy = (lax.axis_index(a) for a in AXES)
    plane = blk * n_gy + gy
    me = sec * n_plane + plane
    n_all = n_sec * n_plane

    copies = [
        pltpu.make_async_copy(src, fields.at[i], in_sem.at[i])
        for i, src in enumerate((kelvin_hbm, co2_hbm, h2o_hbm, soot_hbm))
    ]
    copies.append(pltpu.make_async_copy(order_hbm, order_ref, in_sem.at[4]))
    copies.append(pltpu.make_async_copy(matrix_hbm, matrix, in_sem.at[5]))
    copies.append(pltpu.make_async_copy(tile_hbm, tile_ref, in_sem.at[6]))
    copies.append(pltpu.make_async_copy(live_hbm, live_ref, in_sem.at[7]))
    for copy in copies:
        copy.start()

    def plane_peer(i):
        flat = lax.rem(me + i, n_all)
        return {
            "sec": lax.div(flat, n_plane),
            "blk": lax.rem(lax.div(flat, n_gy), n_blk),
            "gy": lax.rem(flat, n_gy),
        }

    def each(count, body):
        if count <= 32:
            for i in range(1, count):
                body(i)
        else:
            lax.fori_loop(1, count, lambda i, c: (body(i), c)[1], 0)

    barrier = pltpu.get_barrier_semaphore()
    each(
        n_all,
        lambda i: pl.semaphore_signal(
            barrier, inc=1, device_id=plane_peer(i), device_id_type=MESH
        ),
    )

    places = (("sec", sec, n_sec), ("blk", blk, n_blk), ("gy", gy, n_gy))
    landing = (x_in, z_in, y_in)
    leaving = (x_out, z_out, y_out)
    for (_, at, size), land in zip(places, landing):
        for side, edge in ((0, 0), (1, size - 1)):

            @pl.when(at == edge)
            def _(land=land, side=side):
                land[side] = jnp.zeros(land.shape[1:], land.dtype)

    copies[4].wait()
    order = order_ref[...]
    across = cx // BOX
    x_shape = (cx, zones)
    r_shape = (cells // BOX, zones)
    x_at = iota(x_shape, 0)
    r_at = iota(r_shape, 0)
    same_x = lax.rem(order, across) == lax.div(x_at, BOX)
    box_row = lax.div(r_at, cy) * (cy // BOX) + lax.div(lax.rem(r_at, cy), BOX)
    same_r = lax.div(order, across) == box_row
    pick_x = jnp.where(same_x & (lax.rem(x_at, BOX) == 0), 1.0, 0.0).astype(jnp.bfloat16)
    pick_r = same_r & (lax.rem(r_at, BOX) == 0)
    for copy in copies[:4]:
        copy.wait()

    kelvin = fields[0]
    vapour = fields[1] + fields[2]
    soot_kelvin = fields[3] * kelvin
    share = vapour * (VAPOUR_OFFSET + VAPOUR_SLOPE * kelvin) + (
        particulate_attenuation_rate * soot_kelvin * (SHARE_OFFSET + SHARE_SLOPE * kelvin)
    )
    squared = kelvin * kelvin
    emission = radiance_multiplier * (squared * squared) * share
    slabs = emission.reshape(cz // BOX, BOX, cy, cx)
    slabs = (slabs[:, 0] + slabs[:, 1] + slabs[:, 2] + slabs[:, 3]).reshape(cells // BOX, cx)
    box_mean = group_sum(group_sum(slabs, 0), 1) * (1.0 / (BOX * BOX * BOX))

    by_row = jnp.dot(box_mean.astype(jnp.bfloat16), pick_x, preferred_element_type=jnp.float32)
    emitted = jnp.sum(jnp.where(pick_r, by_row, 0.0), axis=0, keepdims=True)
    for r in range(rows):
        gathered[me * rows + r] = emitted[:, r * zone : (r + 1) * zone]

    lane = iota((cells, cx), 1)
    packed = jnp.zeros((cells, cx), jnp.float32)
    for f in range(4):
        field = fields.at[f]
        z_out[0, f] = field[pl.ds(0, cy), :]
        z_out[1, f] = field[pl.ds(cells - cy, cy), :]
        y_out[0, f] = field[pl.ds(0, cz, stride=cy), :]
        y_out[1, f] = field[pl.ds(cy - 1, cz, stride=cy), :]
        packed = jnp.where((lane >> 1) == f, pltpu.roll(field[...], 2 * f + 1, 1), packed)
    x_out[...] = jnp.transpose(packed)[:8]

    pl.semaphore_wait(barrier, n_all - 1)

    def push(start, length, peer, stage):
        block = gathered.at[pl.ds(start, length)]
        pltpu.make_async_remote_copy(
            src_ref=block,
            dst_ref=block,
            send_sem=send_sem.at[stage],
            recv_sem=recv_sem.at[stage],
            device_id=peer,
            device_id_type=MESH,
        ).start()

    def settle(length, sem):
        block = gathered.at[pl.ds(0, length)]
        pltpu.make_async_copy(block, block, sem).wait()

    each(n_all, lambda i: push(me * rows, rows, plane_peer(i), 0))

    def face(which, side):
        axis, at, _ = places[which]
        source = x_out if which == 0 else leaving[which].at[side]
        return pltpu.make_async_remote_copy(
            src_ref=source,
            dst_ref=landing[which].at[1 - side],
            send_sem=face_send.at[which, side],
            recv_sem=face_recv.at[which, 1 - side],
            device_id={axis: at + (2 * side - 1)},
            device_id_type=MESH,
        )

    def has(which, side):
        _, at, size = places[which]
        return at > 0 if side == 0 else at < size - 1

    for which in (1, 2, 0):
        for side in (0, 1):

            @pl.when(has(which, side))
            def _(which=which, side=side):
                face(which, side).start()

    place = iota((cells, cx), 0)
    y_place = lax.rem(place, cy)
    for f in range(4):
        value = fields[f]
        total = jnp.where(place >= cy, pltpu.roll(value, cy, 0), 0.0)
        total += jnp.where(place < cells - cy, pltpu.roll(value, cells - cy, 0), 0.0)
        total += jnp.where(y_place > 0, pltpu.roll(value, 1, 0), 0.0)
        total += jnp.where(y_place < cy - 1, pltpu.roll(value, cells - 1, 0), 0.0)
        total += jnp.where(lane > 0, pltpu.roll(value, 1, 1), 0.0)
        total += jnp.where(lane < cx - 1, pltpu.roll(value, cx - 1, 1), 0.0)
        done[f] = value + diffusion_rates[f] * (total - 6.0 * value)

    for which in (0, 1, 2):
        for side in (0, 1):

            @pl.when(has(which, side))
            def _(which=which, side=side):
                face(which, 1 - side).wait_recv()

    shape = (32, 4 * cx)
    row, column = iota(shape, 0) & 15, iota(shape, 1)
    chosen = ((row < 8) & (column == (row >> 1) * cx) & ((row & 1) == 0)) | (
        (row >= 8) & (column == ((row - 8) >> 1) * cx + cx - 1) & ((row & 1) == 1)
    )
    sides = jnp.concatenate([x_in[0], x_in[1]], axis=0)
    upper = sides.astype(jnp.bfloat16).astype(jnp.float32)
    x_add = lax.dot_general(
        jnp.concatenate([upper, sides - upper], axis=0),
        jnp.where(chosen, 1.0, 0.0),
        TN,
        preferred_element_type=jnp.float32,
    )
    for f in (1, 2, 3, 0):
        rate = diffusion_rates[f]
        out = done.at[f]
        out[...] += rate * x_add[:, f * cx : (f + 1) * cx]
        out[pl.ds(0, cy), :] += rate * z_in[0, f]
        out[pl.ds(cells - cy, cy), :] += rate * z_in[1, f]
        out[pl.ds(0, cz, stride=cy), :] += rate * y_in[0, f]
        out[pl.ds(cy - 1, cz, stride=cy), :] += rate * y_in[1, f]

    spread_x = jnp.where(same_x, 1.0, 0.0).astype(jnp.bfloat16)
    for copy in copies[5:]:
        copy.wait()
    settle((n_all - 1) * rows, recv_sem.at[0])

    absorbed = []
    for r in range(rows):
        total = jnp.zeros((1, zone), jnp.float32)
        for k in range(slots):
            tile = jnp.clip(tile_ref[r, k], 0, gathered.shape[0] - 1)
            picked = jnp.where(k < live_ref[r], gathered[tile], 0.0).astype(jnp.bfloat16)
            total += lax.dot_general(picked, matrix[r, k], NT, preferred_element_type=jnp.float32)
        absorbed.append(total)
    absorbed = jnp.concatenate(absorbed, axis=1)
    high = absorbed.astype(jnp.bfloat16).astype(jnp.float32)
    low = absorbed - high
    both = jnp.concatenate(
        [jnp.where(same_r, high, 0.0), jnp.where(same_r, low, 0.0)], axis=0
    ).astype(jnp.bfloat16)
    carried = lax.dot_general(both, spread_x, NT, preferred_element_type=jnp.float32)
    net = carried[: cells // BOX] + carried[cells // BOX :] - box_mean
    source = jnp.broadcast_to(
        net.reshape(cz // BOX, 1, cy, cx), (cz // BOX, BOX, cy, cx)
    ).reshape(cells, cx)
    done[4] = source
    done[0] += heating_rate * source

    settle((n_all - 1) * rows, send_sem.at[0])
    for which in (0, 1, 2):
        for side in (0, 1):

            @pl.when(has(which, side))
            def _(which=which, side=side):
                face(which, side).wait_send()


def carry(source, *rest):
    outs, sem = rest[:5], rest[5]
    copies = [pltpu.make_async_copy(source.at[i], out, sem.at[i]) for i, out in enumerate(outs)]
    for copy in copies:
        copy.start()
    for copy in copies:
        copy.wait()


def solution(mesh):
    counts = tuple(mesh.shape[a] for a in AXES)

    def local(kelvin, co2, h2o, soot, order, tiles, live, matrix):
        dims = kelvin.shape
        cz, cy, cx = dims
        cells = cz * cy
        rows = matrix.shape[0]
        zone = matrix.shape[2]
        blocks = counts[0] * counts[1] * counts[2] * rows
        flat = [a.reshape(cells, cx) for a in (kelvin, co2, h2o, soot)]
        order = order.reshape(1, -1)
        anywhere = pl.BlockSpec(memory_space=pl.ANY)
        f32 = jnp.float32
        done = pl.pallas_call(
            functools.partial(kernel, dims, counts),
            out_shape=pltpu.VMEM((5, cells, cx), f32),
            in_specs=[anywhere] * 8,
            out_specs=pl.BlockSpec(memory_space=pltpu.VMEM),
            scratch_shapes=[
                pltpu.VMEM((4, cells, cx), f32),
                pltpu.VMEM(order.shape, jnp.int32),
                pltpu.VMEM(matrix.shape, matrix.dtype),
                pltpu.VMEM((blocks, 1, zone), f32),
                pltpu.VMEM((2, 4, cy, cx), f32),
                pltpu.VMEM((2, 4, cz, cx), f32),
                pltpu.VMEM((8, cells), f32),
                pltpu.VMEM((2, 4, cy, cx), f32),
                pltpu.VMEM((2, 4, cz, cx), f32),
                pltpu.VMEM((2, 8, cells), f32),
                pltpu.SMEM(tiles.shape, tiles.dtype),
                pltpu.SMEM(live.shape, live.dtype),
                pltpu.SemaphoreType.DMA((8,)),
                pltpu.SemaphoreType.DMA((3, 2)),
                pltpu.SemaphoreType.DMA((3, 2)),
                pltpu.SemaphoreType.DMA((2,)),
                pltpu.SemaphoreType.DMA((2,)),
            ],
            compiler_params=pltpu.CompilerParams(collective_id=0, has_side_effects=True),
        )(*flat, order, tiles, live, matrix)
        outs = pl.pallas_call(
            carry,
            out_shape=[jax.ShapeDtypeStruct((cells, cx), f32)] * 5,
            in_specs=[anywhere],
            out_specs=[anywhere] * 5,
            scratch_shapes=[
                pltpu.SemaphoreType.DMA((5,)),
            ],
            compiler_params=pltpu.CompilerParams(vmem_limit_bytes=4 << 20),
        )(done)
        return tuple(o.reshape(dims) for o in outs)

    cell = P("blk", "gy", "sec")
    block = P(AXES)
    return jax.shard_map(
        local,
        mesh=mesh,
        in_specs=(cell,) * 4 + (P("sec", "blk", "gy", None), P(AXES, None), block, P(AXES, None, None, None)),
        out_specs=(cell,) * 5,
        check_vma=False,
    )
```
